32 devices in a mesh: bulk: 4 (over y, x), grp: 8 (over z, core).
Axes of the slice: x: 2, y: 2, z: 4, core: 2. Of those that a mesh axis runs over, the one named last changes fastest.
Arguments:
- embeddings: bfloat16 [16384, 768], P(('bulk', 'grp')), may hold values from -6 to 6
- cluster_ids: int32 [16384, 1], P(('bulk', 'grp')), may hold values from 0 to 3; in each aligned block of 512 rows (0 to 511, 512 to 1023, ...) at most 192 rows name the same one
- row_order: int32 [16384], P(('bulk', 'grp')), may hold values from 0 to 16383, each once
Outputs:
- earlier_max: float32 [16384], P(('bulk', 'grp'))
The draws below stay inside these ranges and needn't reach their ends.
Inputs may be any that keep to these rules, and one draw needn't show every extreme that they name: `cluster_ids`: the rows of one device name any one cluster at most 192 times; some cluster is named exactly 192 times by some device's rows.
All inputs are finite; a program needn't handle non-finite values.
Results may differ from the reference program's by a relative error of at most 0.0013.
Values may be sent and summed in bfloat16 or wider, within the bound.
No kernel may reach another device: no remote copies, remote signals or barrier semaphores. Data moves between devices by JAX's collectives and lax.ppermute only.
A program may use at most 64 MiB of HBM per device.

```python
import math
import jax
import jax.numpy as jnp
import numpy as np
from jax import lax

D = 768
ROWS_DEV = 512
CAP = 192
CLUSTERS = 4
ROWS = 16384
N_BULK = 4
N_GRP = 8


def levels(key, shape, cuts, smallest, high):
    gain = 1.0
    for dim, shards_of in cuts:
        heights = jax.random.uniform(jax.random.fold_in(jax.random.fold_in(key, 6), dim), (shards_of,), jnp.float32, smallest / len(cuts), high / len(cuts))
        gain = gain * jnp.repeat(jnp.exp(heights), shape[dim] // shards_of).reshape((-1,) + (1,) * (len(shape) - 1 - dim))
    return gain


def deal_out(own_key, own, number, rows, number_of, top, reach, skew):
    sequence = jax.random.permutation(own_key, number_of)
    packed, ordinary = portions_of(number_of, rows * top, reach, skew, True), portions_of(number_of, rows * top, reach, skew, False)
    places = jnp.arange(number_of)

    def named(lengths, turn):
        used = int((lengths > 0).sum())
        fixed = max(1, used // 4)
        passed = fixed + (places - fixed + turn * (used - fixed)) % max(1, number_of - fixed)
        return jnp.zeros((number_of,), jnp.int32).at[sequence[jnp.where(places < fixed, places, passed)]].set(jnp.asarray(lengths, jnp.int32))

    lengths = jnp.where(number % 4 == 0, named(packed, number // 4), named(ordinary, number - number // 4 - 1))
    mixed = jax.random.permutation(jax.random.fold_in(own, 3), number_of)
    giver, receiver = mixed[0:number_of // 2 * 2:2], mixed[1:number_of // 2 * 2:2]
    slack = jnp.minimum(lengths[giver] - 1, reach - lengths[receiver]) // 2
    slack = jnp.where((giver == sequence[0]) | (receiver == sequence[0]) | (lengths[receiver] == 0), 0, jnp.maximum(slack, 0))
    passed = jax.random.randint(jax.random.fold_in(own, 4), (number_of // 2,), 0, 1 << 20) % (slack + 1)
    lengths = lengths.at[giver].add(-passed).at[receiver].add(passed)
    items = jnp.searchsorted(jnp.cumsum(lengths), jnp.arange(rows * top), side="right").astype(jnp.int32)
    listing = items.reshape(top, rows).T
    listing = listing[jax.random.permutation(jax.random.fold_in(own, 1), rows)]
    turn = jax.random.randint(jax.random.fold_in(own, 2), (rows, 1), 0, top)
    return jnp.take_along_axis(listing, (jnp.arange(top)[None, :] + turn) % top, axis=1)


def portions_of(count, total, bound, lean, full):
    weights = [(1 << 20) // math.isqrt(grade ** lean) + 1 for grade in range(1, count + 1)]
    largest = bound if full else min(bound, max(-(-total // count), total * weights[0] // sum(weights)))
    least = 1 if total - largest >= count - 1 else 0
    given, spare = [largest] + [least] * (count - 1), total - largest - least * (count - 1)
    while spare > 0:
        movable = [i for i in range(1, count) if given[i] < largest] or [i for i in range(1, count) if given[i] < bound]
        mass, left = sum([weights[i] for i in movable]), spare
        for i in movable:
            extra = min(bound - given[i], max(1, left * weights[i] // mass), spare)
            given[i] = given[i] + extra
            spare = spare - extra
    return np.array(given)


def noise(stream_key, extent, spread, limit, shards=(), kind=jnp.bfloat16):
    drawn = jax.random.normal(stream_key, extent, jnp.float32) * spread
    if len(shards) > 0:
        drawn = levels(stream_key, extent, shards, -0.22, 0.18) * drawn
    return jnp.clip(drawn, min=-limit, max=limit).astype(kind)


def setup_inputs(seed: int = 0) -> dict:
    keys = jax.random.split(jax.random.key(seed), 4)
    embeddings = noise(keys[0], (ROWS, D), 1.0, 6.0, ((0, 32),))
    cluster_ids_keys = jax.random.split(jax.random.fold_in(keys[1], 1), ROWS // ROWS_DEV)
    cluster_ids_turns = jax.random.permutation(jax.random.fold_in(keys[1], 3), ROWS // ROWS_DEV)
    cluster_ids = jax.vmap(lambda own, number: deal_out(jax.random.fold_in(keys[1], 2), own, number, ROWS_DEV, CLUSTERS, 1, CAP, 2))(cluster_ids_keys, cluster_ids_turns).reshape((ROWS, 1))
    row_order = jax.random.permutation(keys[2], ROWS).astype(jnp.int32)
    return dict(embeddings=embeddings, cluster_ids=cluster_ids, row_order=row_order)


def reference(embeddings, cluster_ids, row_order):
    values = embeddings.astype(jnp.float32)
    unit = (values * lax.rsqrt(lax.optimization_barrier(jnp.sum(values * values, axis=1, keepdims=True)) + 1e-06)).astype(jnp.bfloat16)
    total = embeddings.shape[0]
    cluster = cluster_ids[:, 0].astype(jnp.int32)
    keyed = cluster * total + row_order.astype(jnp.int32)
    permuted = jnp.argsort(keyed).astype(jnp.int32)
    sorted_unit = unit[permuted]
    sorted_cluster = cluster[permuted]
    counts = lax.optimization_barrier(jnp.sum((cluster[:, None] == jnp.arange(N_BULK, dtype=jnp.int32)[None, :]).astype(jnp.int32), axis=0))
    starts = (jnp.cumsum(counts) - counts).astype(jnp.int32)
    biggest = N_BULK * N_GRP * CAP
    padded = jnp.concatenate([sorted_unit, jnp.zeros((biggest, sorted_unit.shape[1]), jnp.bfloat16)], axis=0)
    places = jnp.arange(biggest, dtype=jnp.int32)

    def one_cluster(index):
        block = lax.dynamic_slice_in_dim(padded, starts[index].astype(jnp.int32), biggest, 0)
        gram = jnp.dot(block, block.T, preferred_element_type=jnp.float32)
        usable = (places[None, :] < places[:, None]) & (places[None, :] < counts[index])
        return lax.optimization_barrier(jnp.max(jnp.where(usable, gram, jnp.float32(-1.0)), axis=1))
    bests = lax.map(one_cluster, jnp.arange(N_BULK, dtype=jnp.int32))
    position = jnp.arange(total, dtype=jnp.int32) - starts[sorted_cluster]
    sorted_result = bests[sorted_cluster, position]
    return jnp.zeros((total,), jnp.float32).at[permuted].set(sorted_result)
```

```python
import functools

import jax
import jax.numpy as jnp
from jax import lax
from jax.experimental import pallas as pl
from jax.experimental.pallas import tpu as pltpu
from jax.sharding import PartitionSpec as P

F32 = jnp.float32
BF16 = jnp.bfloat16
KEYS = 16
FRONT = 288
VMEM_LIMIT = 32 * 1024 * 1024


def plane_pairs(planes):
    load = {}
    sent, got = [0] * planes, [0] * planes

    def links(a, b):
        step = 1 if b > a else -1
        return [(p, p + step) for p in range(a, b, step)]

    chosen = []
    for distance in range(planes - 1, 0, -1):
        for low in range(planes - distance):
            options = []
            for a, b in ((low + distance, low), (low, low + distance)):
                path = links(a, b)
                worst = max(load.get(link, 0) for link in path)
                total = sum(load.get(link, 0) for link in path)
                options.append((worst, total, got[b], sent[a], len(options), a, b))
            a, b = min(options)[-2:]
            for link in links(a, b):
                load[link] = load.get(link, 0) + 1
            sent[a] += 1
            got[b] += 1
            chosen.append((a, b))
    rounds = []
    for a, b in chosen:
        for members in rounds:
            if all(a != c and b != d for c, d in members):
                members.append((a, b))
                break
        else:
            rounds.append([(a, b)])
    return rounds


def digits(ref, first):
    keys = ref[pl.ds(first, KEYS), :].astype(F32)
    order = keys[0:1] + 128.0 * keys[1:2] + 16384.0 * keys[2:3]
    return order, keys[3:4]


def columns(row, length):
    return jnp.transpose(jnp.broadcast_to(row, (8, row.shape[1])))[:length, 0:1]


def pack_kernel(values_ref, cluster_ref, order_ref, full_ref, *part_refs):
    rows, width = values_ref.shape
    fronts, backs = part_refs[0::2], part_refs[1::2]
    big = rows - backs[0].shape[0]
    order = order_ref[...]
    kept = [order & 127, (order >> 7) & 127, order >> 14, cluster_ref[...] + 1]
    kept += [jnp.zeros_like(order)] * (KEYS - len(kept))
    keys = jnp.concatenate(kept, axis=0).astype(F32).astype(BF16)
    if width > rows:
        keys = jnp.concatenate([keys, jnp.zeros((KEYS, width - rows), BF16)], axis=1)
    values = values_ref[...].astype(F32)
    unit = (values * lax.rsqrt(jnp.sum(values * values, axis=1, keepdims=True) + 1e-06)).astype(BF16)
    full_ref[0:rows, :] = unit
    full_ref[rows : rows + KEYS, :] = keys
    for front in fronts:
        front[0:big, :] = unit[:big]
        front[big : big + KEYS, :] = keys
    for back in backs:
        back[...] = unit[big:]


def pack(values, cluster, order, big, copies):
    rows, width = values.shape
    sizes = [rows + KEYS] + [big + KEYS, rows - big] * copies
    out = pl.pallas_call(
        pack_kernel,
        out_shape=[jax.ShapeDtypeStruct((size, width), BF16) for size in sizes],
        compiler_params=pltpu.CompilerParams(vmem_limit_bytes=VMEM_LIMIT),
        name="pack",
    )(values, cluster, order)
    return out[0], out[1::2], out[2::2]


def pair_kernel(plan, *refs):
    n_arrays, ms, ps, sides = plan
    arrays, best_ref, out_ref = refs[:n_arrays], refs[n_arrays], refs[n_arrays + 1]
    out_ref[...] = best_ref[...]
    keys = {}
    for _, _, _, keyed, first, _, _ in ms + ps:
        if (keyed, first) not in keys:
            keys[keyed, first] = digits(arrays[keyed], first)
    tiles = []
    for p, start, count, keyed, first, at, line in ps:
        order, cluster = keys[keyed, first]
        tile = min(256, count)
        for t in range(0, count, tile):
            span = slice(at + t, at + t + tile)
            rows = slice(start + t, start + t + tile)
            tiles.append([p, rows, tile, order[:, span], cluster[:, span], line, span, jnp.full((8, tile), -1.0, F32)])
    for (m, start, count, keyed, first, at, line), both in zip(ms, sides):
        order, cluster = (columns(row[:, at : at + count], count) for row in keys[keyed, first])
        m_rows = arrays[m][start : start + count, :]
        m_best = jnp.full((count, 128), -1.0, F32)
        for held in tiles:
            p, rows, tile, p_order, p_cluster, _, _, p_best = held
            scores = lax.dot_general(
                m_rows, arrays[p][rows, :], (((1,), (1,)), ((), ())), preferred_element_type=F32
            )
            scores = jnp.where(cluster == p_cluster, scores, -1.0)
            later = order > p_order
            mine = jnp.where(later, scores, -1.0)
            for c in range(0, tile, 128):
                m_best = jnp.maximum(m_best, mine[:, c : c + 128])
            if both:
                other = jnp.where(later, -1.0, scores).reshape(count // 8, 8, tile)
                held[-1] = jnp.maximum(p_best, jnp.max(other, axis=0))
        m_line = jnp.max(jnp.transpose(m_best), axis=0, keepdims=True)
        span = slice(at, at + count)
        out_ref[line : line + 1, span] = jnp.maximum(out_ref[line : line + 1, span], m_line)
    if any(sides):
        for *_, line, span, p_best in tiles:
            p_line = jnp.max(p_best, axis=0, keepdims=True)
            out_ref[line : line + 1, span] = jnp.maximum(out_ref[line : line + 1, span], p_line)


def fold(best, ms, ps, name):
    arrays = []

    def place(array):
        for at, held in enumerate(arrays):
            if held is array:
                return at
        arrays.append(array)
        return len(arrays) - 1

    def planned(piece):
        return place(piece[0]), *piece[1:3], place(piece[3]), *piece[4:7]

    plan = ([planned(piece) for piece in ms], [planned(piece) for piece in ps], [piece[-1] for piece in ms])
    return pl.pallas_call(
        functools.partial(pair_kernel, (len(arrays), *plan)),
        out_shape=jax.ShapeDtypeStruct(best.shape, F32),
        compiler_params=pltpu.CompilerParams(vmem_limit_bytes=VMEM_LIMIT),
        cost_estimate=pl.CostEstimate(flops=0, bytes_accessed=0, transcendentals=0),
        name=name,
    )(*arrays, best)


def after(x, *others):
    return lax.optimization_barrier((x, *others))[0]


def on_device(embeddings, cluster_ids, row_order):
    rows = embeddings.shape[0]
    n_bulk, n_grp = lax.axis_size("bulk"), lax.axis_size("grp")
    planes = n_grp // 2
    axes = ("bulk", "grp")

    def bulk_move(x, mask):
        pairs = [(b * n_grp + g, (b ^ mask) * n_grp + g) for b in range(n_bulk) for g in range(n_grp)]
        return lax.ppermute(x, axes, pairs)

    def core_move(x):
        pairs = [(b * n_grp + g, b * n_grp + (g ^ 1)) for b in range(n_bulk) for g in range(n_grp)]
        return lax.ppermute(x, axes, pairs)

    def plane_move(x, members):
        pairs = [
            (b * n_grp + 2 * s + c, b * n_grp + 2 * d + c) for b in range(n_bulk) for s, d in members for c in range(2)
        ]
        return lax.ppermute(x, axes, pairs)

    rounds = plane_pairs(planes)
    n_rounds = len(rounds)
    big = FRONT * rows // 512
    small = rows - big
    half = rows // 2
    last = n_bulk - 1
    full, fronts, backs = pack(embeddings, cluster_ids.reshape(1, rows), row_order.reshape(1, rows), big, n_rounds)

    own_lines = -(-(1 + n_rounds + n_bulk) // 8) * 8
    own_line, z_line = 0, lambda k: 1 + k
    p_line = lambda j: 1 + n_rounds + j
    t_line, tz_line = own_lines, lambda k: own_lines + 1 + k
    best = jnp.full((own_lines + -(-(1 + n_rounds) // 8) * 8, rows), -1.0, F32)

    def whole(x, line):
        return x, 0, rows, x, rows, 0, line

    twin = core_move(full)
    z_front = [plane_move(x, members) for x, members in zip(fronts, rounds)]
    bulk = [full] + [bulk_move(full, mask) for mask in range(1, last)]
    same = [whole(full, own_line) + (False,), whole(twin, t_line) + (False,)]
    blocks = [whole(bulk[j], p_line(j)) for j in range(last)]
    best = fold(best, same, blocks[:1], "own")
    d_top = bulk_move(bulk[1][:half], last ^ 1)
    d_end = bulk_move(bulk[last ^ 1][half:], 1)
    z_back = [plane_move(after(x, z_front[0], twin, *bulk[1:]), members) for x, members in zip(backs, rounds)]
    z_front_twin = core_move(jnp.concatenate([after(z_front[0], *bulk[1:])] + z_front[1:], axis=0))
    best = fold(best, same, blocks[1:], "plane")
    far = [(d_top, 0, half, d_end, half, 0, p_line(last)), (d_end, 0, half, d_end, half, half, p_line(last))]
    firsts, seconds = [], []
    for k in range(n_rounds):
        lead = k * (big + KEYS)
        firsts.append((z_front[k], 0, big, z_front[k], big, 0, z_line(k), True))
        firsts.append((z_front_twin, lead, big, z_front_twin, lead + big, 0, tz_line(k), True))
    best = fold(best, firsts, blocks, "front")
    best = fold(best, same + firsts, far, "far")
    z_back = [after(z_back[0], best)] + z_back[1:]
    z_back_twin = core_move(jnp.concatenate(z_back, axis=0))
    for k in range(n_rounds):
        lead = k * (big + KEYS)
        seconds.append((z_back[k], 0, small, z_front[k], big, big, z_line(k), True))
        seconds.append((z_back_twin, k * small, small, z_front_twin, lead + big, big, tz_line(k), True))
    best = fold(best, seconds, blocks + far, "back")

    from_twin = core_move(best[own_lines:])
    parts = [best[own_line], best[p_line(0)], from_twin[0]]
    parts += [bulk_move(best[p_line(j)], j) for j in range(1, n_bulk)]
    plane = lax.axis_index("grp") // 2
    for k, members in enumerate(rounds):
        total = jnp.maximum(best[z_line(k)], from_twin[1 + k])
        part = plane_move(total, [(d, s) for s, d in members])
        senders = [s for s, _ in members]
        if len(senders) < planes:
            sent = functools.reduce(jnp.logical_or, [plane == s for s in senders])
            part = jnp.where(sent, part, -1.0)
        parts.append(part)
    return functools.reduce(jnp.maximum, parts)


def solution(mesh):
    return jax.shard_map(
        on_device,
        mesh=mesh,
        in_specs=(P(("bulk", "grp"), None), P(("bulk", "grp"), None), P(("bulk", "grp"))),
        out_specs=P(("bulk", "grp")),
        check_vma=False,
    )
```

```python
import functools

import jax
import jax.numpy as jnp
from jax import lax
from jax.experimental import pallas as pl
from jax.experimental.pallas import tpu as pltpu
from jax.sharding import PartitionSpec as P

F32 = jnp.float32
BF16 = jnp.bfloat16
KEYS = 16
VMEM_LIMIT = 32 * 1024 * 1024


def plane_rounds(planes):
    rounds = [[(z, (z - k) % planes) for z in range(planes)] for k in range(1, (planes + 1) // 2)]
    if planes % 2 == 0:
        half = planes // 2
        rounds.append([(z, z + half) if z % 2 == 0 else (z + half, z) for z in range(half)])
    return rounds


def digits(ref, first):
    keys = ref[pl.ds(first, KEYS), :].astype(F32)
    order = keys[0:1] + 128.0 * keys[1:2] + 16384.0 * keys[2:3]
    return order, keys[3:4]


def columns(row, length):
    return jnp.transpose(jnp.broadcast_to(row, (8, row.shape[1])))[:length, 0:1]


def pack_kernel(values_ref, marks_ref, full_ref):
    rows, width = values_ref.shape
    values = values_ref[...].astype(F32)
    unit = values * lax.rsqrt(jnp.sum(values * values, axis=1, keepdims=True) + 1e-06)
    full_ref[0:rows, :] = unit.astype(BF16)
    order, cluster = marks_ref[0:1, :], marks_ref[1:2, :]
    kept = [order & 127, (order >> 7) & 127, order >> 14, cluster + 1]
    kept += [jnp.zeros_like(order)] * (KEYS - len(kept))
    keys = jnp.concatenate(kept, axis=0).astype(F32).astype(BF16)
    if width > rows:
        keys = jnp.concatenate([keys, jnp.zeros((KEYS, width - rows), BF16)], axis=1)
    full_ref[rows : rows + KEYS, :] = keys


def pack(values, marks):
    rows, width = values.shape
    return pl.pallas_call(
        pack_kernel,
        out_shape=jax.ShapeDtypeStruct((rows + KEYS, width), BF16),
        compiler_params=pltpu.CompilerParams(vmem_limit_bytes=VMEM_LIMIT),
        name="pack",
    )(values, marks)


def row_range(arrays, parts, low, count):
    taken = []
    for array, first, rows in parts:
        begin, end = max(low, 0), min(low + count, rows)
        if begin < end:
            taken.append((array, slice(first + begin, first + end)))
        low -= rows

    def read():
        held = [arrays[array][rows, :] for array, rows in taken]
        return held[0] if len(held) == 1 else jnp.concatenate(held, axis=0)

    return read


def pair_kernel(plan, *refs):
    n_arrays, ms, ps, sides = plan
    arrays, best_ref, out_ref = refs[:n_arrays], refs[n_arrays], refs[n_arrays + 1]
    out_ref[...] = best_ref[...]
    keys = {}
    for keyed, first in [piece[3:5] for piece in ms] + [block[1:3] for block in ps]:
        if (keyed, first) not in keys:
            keys[keyed, first] = digits(arrays[keyed], first)
    tiles = []
    for parts, keyed, first, line in ps:
        order, cluster = keys[keyed, first]
        rows = sum(count for _, _, count in parts)
        tile = min(256, rows)
        for low in range(0, rows, tile):
            span = slice(low, low + tile)
            tiles.append([row_range(arrays, parts, low, tile), order[:, span], cluster[:, span], line, span, tile])
            tiles[-1].append(jnp.full((8, tile), -1.0, F32))
    for (m, start, count, keyed, first, at, line), both in zip(ms, sides):
        order, cluster = (columns(row[:, at : at + count], count) for row in keys[keyed, first])
        m_rows = arrays[m][start : start + count, :]
        m_best = jnp.full((count, 128), -1.0, F32)
        for held in tiles:
            p_rows, p_order, p_cluster, _, _, tile, p_best = held
            scores = lax.dot_general(m_rows, p_rows(), (((1,), (1,)), ((), ())), preferred_element_type=F32)
            scores = jnp.where(cluster == p_cluster, scores, -1.0)
            later = order > p_order
            mine = jnp.where(later, scores, -1.0)
            for c in range(0, tile, 128):
                m_best = jnp.maximum(m_best, mine[:, c : c + 128])
            if both:
                other = jnp.where(later, -1.0, scores).reshape(count // 8, 8, tile)
                held[-1] = jnp.maximum(p_best, jnp.max(other, axis=0))
        m_line = jnp.max(jnp.transpose(m_best), axis=0, keepdims=True)
        span = slice(at, at + count)
        out_ref[line : line + 1, span] = jnp.maximum(out_ref[line : line + 1, span], m_line)
    if any(sides):
        for _, _, _, line, span, _, p_best in tiles:
            p_line = jnp.max(p_best, axis=0, keepdims=True)
            out_ref[line : line + 1, span] = jnp.maximum(out_ref[line : line + 1, span], p_line)


def fold(best, ms, ps, name):
    arrays = []

    def place(array):
        for at, held in enumerate(arrays):
            if held is array:
                return at
        arrays.append(array)
        return len(arrays) - 1

    m_plan = [(place(m[0]), *m[1:3], place(m[3]), *m[4:7]) for m in ms]
    p_plan = [([(place(a), *rest) for a, *rest in p[0]], place(p[1]), *p[2:]) for p in ps]
    plan = (m_plan, p_plan, [m[-1] for m in ms])
    return pl.pallas_call(
        functools.partial(pair_kernel, (len(arrays), *plan)),
        out_shape=jax.ShapeDtypeStruct(best.shape, F32),
        compiler_params=pltpu.CompilerParams(vmem_limit_bytes=VMEM_LIMIT),
        cost_estimate=pl.CostEstimate(flops=0, bytes_accessed=0, transcendentals=0),
        name=name,
    )(*arrays, best)


def after(x, *others):
    return lax.optimization_barrier((x, *others))[0]


def on_device(embeddings, cluster_ids, row_order):
    rows = embeddings.shape[0]
    n_bulk, n_grp = lax.axis_size("bulk"), lax.axis_size("grp")
    planes = n_grp // 2
    axes = ("bulk", "grp")

    def bulk_move(x, mask):
        pairs = [(b * n_grp + g, (b ^ mask) * n_grp + g) for b in range(n_bulk) for g in range(n_grp)]
        return lax.ppermute(x, axes, pairs)

    def core_move(x):
        pairs = [(b * n_grp + g, b * n_grp + (g ^ 1)) for b in range(n_bulk) for g in range(n_grp)]
        return lax.ppermute(x, axes, pairs)

    def plane_move(x, members):
        pairs = [
            (b * n_grp + 2 * s + c, b * n_grp + 2 * d + c) for b in range(n_bulk) for s, d in members for c in range(2)
        ]
        return lax.ppermute(x, axes, pairs)

    rounds = plane_rounds(planes)
    n_rounds = len(rounds)
    half, near_cut = rows // 2, 5 * rows // 8
    last = n_bulk - 1
    full = pack(embeddings, jnp.stack([row_order, cluster_ids.reshape(rows)]))

    own_line, t_line = 0, 1
    z_line, tz_line = lambda k: 2 + 2 * k, lambda k: 3 + 2 * k
    p_line = lambda j: 2 + 2 * n_rounds + j
    best = jnp.full((-(-p_line(n_bulk) // 8) * 8, rows), -1.0, F32)

    def whole(x, line, both):
        return x, 0, rows, x, rows, 0, line, both

    def block(x, line):
        return [(x, 0, rows)], x, rows, line

    def go_home(lines, k):
        back = {(d, s) for s, d in rounds[k]}
        if len(back) < planes:
            back |= {(s, d) for d, s in back}
        return plane_move(lines, sorted(back))

    twin = core_move(full)
    z = [plane_move(full, members) for members in rounds]
    bulk = [bulk_move(full, mask) for mask in range(1, last)]
    same = [whole(full, own_line, False), whole(twin, t_line, False)]
    blocks = [block(full, p_line(0))]
    best = fold(best, same, blocks, "own")
    bulk = [full] + [after(x, best) for x in bulk]
    d_top = bulk_move(bulk[1][:near_cut], last ^ 1)
    d_end = bulk_move(bulk[last ^ 1][near_cut:], 1)
    k = n_rounds - 1
    z_twin = [(core_move(x[:half]), core_move(x[half:])) for x in z[:k]]
    near = [block(bulk[j], p_line(j)) for j in range(1, last)]
    far = [([(d_top, 0, near_cut), (d_end, 0, rows - near_cut)], d_end, rows - near_cut, p_line(last))]
    most = []
    for r in range(k):
        top, end = z_twin[r]
        most.append(whole(z[r], z_line(r), True))
        most.append((end, 0, half, end, half, half, tz_line(r), True))
        most.append((top, 0, half, end, half, 0, tz_line(r), True))
    best = fold(best, same, near, "near")
    best = fold(best, most, blocks + near, "column")
    best = fold(best, same + most, far, "far")

    parts = [go_home(best[z_line(r) : tz_line(r) + 1], r) for r in range(k)]
    blocks += near + far
    z_last = after(z[k], best)
    z_top, z_end = core_move(z_last[:half]), core_move(z_last[half:])
    best = fold(best, [whole(z_last, z_line(k), True)], blocks, "last")
    best = fold(best, [(z_end, 0, half, z_end, half, half, tz_line(k), True)], blocks, "end")
    parts = [after(x, best) for x in parts]
    best = fold(after(best, *parts), [(z_top, 0, half, z_end, half, 0, tz_line(k), True)], blocks, "top")

    parts.append(go_home(best[z_line(k) : tz_line(k) + 1], k))
    both = functools.reduce(jnp.maximum, parts, best[own_line : t_line + 1])
    mine = best[p_line(0)]
    for j in range(1, n_bulk):
        mine = jnp.maximum(mine, bulk_move(best[p_line(j)], j))
    return jnp.maximum(jnp.maximum(both[0], core_move(both[1])), mine)


def solution(mesh):
    return jax.shard_map(
        on_device,
        mesh=mesh,
        in_specs=(P(("bulk", "grp"), None), P(("bulk", "grp"), None), P(("bulk", "grp"))),
        out_specs=P(("bulk", "grp")),
        check_vma=False,
    )
```

```python
import functools

import jax
import jax.numpy as jnp
from jax import lax
from jax.experimental import pallas as pl
from jax.experimental.pallas import tpu as pltpu
from jax.sharding import PartitionSpec as P

F32 = jnp.float32
BF16 = jnp.bfloat16
KEYS = 16
PARTS = 4
VMEM_LIMIT = 32 * 1024 * 1024


def plane_rounds(planes):
    rounds = [[(z, (z - k) % planes) for z in range(planes)] for k in range(1, (planes + 1) // 2)]
    if planes % 2 == 0:
        half = planes // 2
        rounds.append([(z, z + half) if z % 2 == 0 else (z + half, z) for z in range(half)])
    return rounds


def digits(ref, first):
    keys = ref[pl.ds(first, KEYS), :].astype(F32)
    order = keys[0:1] + 128.0 * keys[1:2] + 16384.0 * keys[2:3]
    return order, keys[3:4]


def columns(row, length):
    return jnp.transpose(jnp.broadcast_to(row, (8, row.shape[1])))[:length, 0:1]


def pack_kernel(values_ref, cluster_ref, order_ref, full_ref, values, cluster, order, sems):
    rows, width = values_ref.shape
    step = rows // PARTS
    spans = [pl.ds(i * step, step) for i in range(PARTS)]
    copies = [pltpu.make_async_copy(values_ref.at[span], values.at[span], sems.at[i]) for i, span in enumerate(spans)]
    copies.append(pltpu.make_async_copy(cluster_ref, cluster, sems.at[PARTS]))
    copies.append(pltpu.make_async_copy(order_ref, order, sems.at[PARTS + 1]))
    for copy in copies:
        copy.start()
    for i in range(PARTS):
        copies[i].wait()
        part = values[i * step : (i + 1) * step, :].astype(F32)
        unit = part * lax.rsqrt(jnp.sum(part * part, axis=1, keepdims=True) + 1e-06)
        full_ref[i * step : (i + 1) * step, :] = unit.astype(BF16)
    copies[PARTS].wait()
    copies[PARTS + 1].wait()
    orders = order[...]
    kept = [orders & 127, (orders >> 7) & 127, orders >> 14, cluster[...] + 1]
    kept += [jnp.zeros_like(orders)] * (KEYS - len(kept))
    keys = jnp.concatenate(kept, axis=0).astype(F32).astype(BF16)
    if width > rows:
        keys = jnp.concatenate([keys, jnp.zeros((KEYS, width - rows), BF16)], axis=1)
    full_ref[rows : rows + KEYS, :] = keys


def pack(values, cluster, order):
    rows, width = values.shape
    held = [pltpu.with_memory_space_constraint(x, pltpu.HBM) for x in (values, cluster, order)]
    return pl.pallas_call(
        pack_kernel,
        out_shape=jax.ShapeDtypeStruct((rows + KEYS, width), BF16),
        in_specs=[pl.BlockSpec(memory_space=pltpu.HBM)] * 3,
        scratch_shapes=[
            pltpu.VMEM(values.shape, BF16),
            pltpu.VMEM(cluster.shape, jnp.int32),
            pltpu.VMEM(order.shape, jnp.int32),
            pltpu.SemaphoreType.DMA((PARTS + 2,)),
        ],
        compiler_params=pltpu.CompilerParams(vmem_limit_bytes=VMEM_LIMIT),
        name="pack",
    )(*held)


def row_range(arrays, parts, low, count):
    taken = []
    for array, first, rows in parts:
        begin, end = max(low, 0), min(low + count, rows)
        if begin < end:
            taken.append((array, slice(first + begin, first + end)))
        low -= rows

    def read():
        held = [arrays[array][rows, :] for array, rows in taken]
        return held[0] if len(held) == 1 else jnp.concatenate(held, axis=0)

    return read


def pair_kernel(plan, *refs):
    n_arrays, ms, ps, sides = plan
    arrays, best_ref, out_ref = refs[:n_arrays], refs[n_arrays], refs[n_arrays + 1]
    out_ref[...] = best_ref[...]
    keys = {}
    for keyed, first in [piece[3:5] for piece in ms] + [block[1:3] for block in ps]:
        if (keyed, first) not in keys:
            keys[keyed, first] = digits(arrays[keyed], first)
    tiles = []
    for parts, keyed, first, line in ps:
        order, cluster = keys[keyed, first]
        rows = sum(count for _, _, count in parts)
        tile = min(256, rows)
        for low in range(0, rows, tile):
            span = slice(low, low + tile)
            tiles.append([row_range(arrays, parts, low, tile), order[:, span], cluster[:, span], line, span, tile])
            tiles[-1].append(jnp.full((8, tile), -1.0, F32))
    for (m, start, count, keyed, first, at, line), both in zip(ms, sides):
        order, cluster = (columns(row[:, at : at + count], count) for row in keys[keyed, first])
        m_rows = arrays[m][start : start + count, :]
        m_best = jnp.full((count, 128), -1.0, F32)
        for held in tiles:
            p_rows, p_order, p_cluster, _, _, tile, p_best = held
            scores = lax.dot_general(m_rows, p_rows(), (((1,), (1,)), ((), ())), preferred_element_type=F32)
            scores = jnp.where(cluster == p_cluster, scores, -1.0)
            later = order > p_order
            mine = jnp.where(later, scores, -1.0)
            for c in range(0, tile, 128):
                m_best = jnp.maximum(m_best, mine[:, c : c + 128])
            if both:
                other = jnp.where(later, -1.0, scores).reshape(count // 8, 8, tile)
                held[-1] = jnp.maximum(p_best, jnp.max(other, axis=0))
        m_line = jnp.max(jnp.transpose(m_best), axis=0, keepdims=True)
        span = slice(at, at + count)
        out_ref[line : line + 1, span] = jnp.maximum(out_ref[line : line + 1, span], m_line)
    if any(sides):
        for _, _, _, line, span, _, p_best in tiles:
            p_line = jnp.max(p_best, axis=0, keepdims=True)
            out_ref[line : line + 1, span] = jnp.maximum(out_ref[line : line + 1, span], p_line)


def fold(best, ms, ps, name):
    arrays = []

    def place(array):
        for at, held in enumerate(arrays):
            if held is array:
                return at
        arrays.append(array)
        return len(arrays) - 1

    m_plan = [(place(m[0]), *m[1:3], place(m[3]), *m[4:7]) for m in ms]
    p_plan = [([(place(a), *rest) for a, *rest in p[0]], place(p[1]), *p[2:]) for p in ps]
    plan = (m_plan, p_plan, [m[-1] for m in ms])
    return pl.pallas_call(
        functools.partial(pair_kernel, (len(arrays), *plan)),
        out_shape=jax.ShapeDtypeStruct(best.shape, F32),
        compiler_params=pltpu.CompilerParams(vmem_limit_bytes=VMEM_LIMIT),
        cost_estimate=pl.CostEstimate(flops=0, bytes_accessed=0, transcendentals=0),
        name=name,
    )(*arrays, best)


def after(x, *others):
    return lax.optimization_barrier((x, *others))[0]


def on_device(embeddings, cluster_ids, row_order):
    rows = embeddings.shape[0]
    n_bulk, n_grp = lax.axis_size("bulk"), lax.axis_size("grp")
    planes = n_grp // 2
    axes = ("bulk", "grp")

    def bulk_move(x, mask):
        pairs = [(b * n_grp + g, (b ^ mask) * n_grp + g) for b in range(n_bulk) for g in range(n_grp)]
        return lax.ppermute(x, axes, pairs)

    def core_move(x):
        pairs = [(b * n_grp + g, b * n_grp + (g ^ 1)) for b in range(n_bulk) for g in range(n_grp)]
        return lax.ppermute(x, axes, pairs)

    def plane_move(x, members):
        pairs = [
            (b * n_grp + 2 * s + c, b * n_grp + 2 * d + c) for b in range(n_bulk) for s, d in members for c in range(2)
        ]
        return lax.ppermute(x, axes, pairs)

    rounds = plane_rounds(planes)
    n_rounds = len(rounds)
    half, near_cut, cut = rows // 2, rows // 2, 3 * rows // 8
    last = n_bulk - 1
    full = pack(embeddings, cluster_ids.reshape(1, rows), row_order.reshape(1, rows))

    own_line, t_line = 0, 1
    z_line, tz_line = lambda k: 2 + 2 * k, lambda k: 3 + 2 * k
    p_line = lambda j: 2 + 2 * n_rounds + j
    best = jnp.full((-(-p_line(n_bulk) // 8) * 8, rows), -1.0, F32)

    def whole(x, line, both):
        return x, 0, rows, x, rows, 0, line, both

    def block(x, line):
        return [(x, 0, rows)], x, rows, line

    def go_home(lines, k):
        back = {(d, s) for s, d in rounds[k]}
        if len(back) < planes:
            back |= {(s, d) for d, s in back}
        return plane_move(lines, sorted(back))

    twin = core_move(full)
    z = [plane_move(full, members) for members in rounds]
    bulk = [bulk_move(full, mask) for mask in range(1, last)]
    same = [whole(full, own_line, False), whole(twin, t_line, False)]
    blocks = [block(full, p_line(0))]
    best = fold(best, same, blocks, "own")
    bulk = [full] + bulk
    d_top = bulk_move(bulk[1][:near_cut], last ^ 1)
    d_end = bulk_move(bulk[last ^ 1][near_cut:], 1)
    k = n_rounds - 1
    z_twin = [(core_move(x[:cut]), core_move(x[cut:])) for x in z[:k]]
    near = [block(bulk[j], p_line(j)) for j in range(1, last)]
    far = [([(d_top, 0, near_cut), (d_end, 0, rows - near_cut)], d_end, rows - near_cut, p_line(last))]
    most = []
    for r in range(k):
        top, end = z_twin[r]
        most.append(whole(z[r], z_line(r), True))
        most.append((end, 0, rows - cut, end, rows - cut, cut, tz_line(r), True))
        most.append((top, 0, cut, end, rows - cut, 0, tz_line(r), True))
    best = fold(best, same, near, "near")
    best = fold(best, most, blocks + near, "column")
    best = fold(best, same + most, far, "far")

    parts = [go_home(best[z_line(r) : tz_line(r) + 1], r) for r in range(k)]
    blocks += near + far
    z_last = after(z[k], best)
    z_last_twin = core_move(z_last)
    best = fold(best, [whole(z_last, z_line(k), True)], blocks, "last")
    best = fold(best, [whole(z_last_twin, tz_line(k), True)], blocks, "rest")

    parts.append(go_home(best[z_line(k) : tz_line(k) + 1], k))
    both = functools.reduce(jnp.maximum, parts, best[own_line : t_line + 1])
    mine = best[p_line(0)]
    for j in range(1, last):
        mine = jnp.maximum(mine, bulk_move(best[p_line(j)], j))
    mine = jnp.maximum(mine, bulk_move(best, last)[p_line(last)])
    return jnp.maximum(jnp.maximum(both[0], core_move(both[1])), mine)


def solution(mesh):
    return jax.shard_map(
        on_device,
        mesh=mesh,
        in_specs=(P(("bulk", "grp"), None), P(("bulk", "grp"), None), P(("bulk", "grp"))),
        out_specs=P(("bulk", "grp")),
        check_vma=False,
    )
```

```python
import functools

import jax
import jax.numpy as jnp
from jax import lax
from jax.experimental import pallas as pl
from jax.experimental.pallas import tpu as pltpu
from jax.sharding import PartitionSpec as P

F32 = jnp.float32
BF16 = jnp.bfloat16
KEYS = 16
PARTS = 2
VMEM_LIMIT = 32 * 1024 * 1024


def plane_rounds(planes):
    rounds = [[(z, (z - k) % planes) for z in range(planes)] for k in range(1, (planes + 1) // 2)]
    if planes % 2 == 0:
        half = planes // 2
        rounds.append([(z, z + half) if z % 2 == 0 else (z + half, z) for z in range(half)])
    return rounds


def digits(ref, first):
    keys = ref[pl.ds(first, KEYS), :].astype(F32)
    order = keys[0:1] + 128.0 * keys[1:2] + 16384.0 * keys[2:3]
    return order, keys[3:4]


def columns(row, length):
    return jnp.transpose(jnp.broadcast_to(row, (8, row.shape[1])))[:length, 0:1]


def pack_kernel(values_ref, cluster_ref, order_ref, full_ref, values, cluster, order, sems):
    rows, width = values_ref.shape
    step = rows // PARTS
    spans = [pl.ds(i * step, step) for i in range(PARTS)]
    copies = [pltpu.make_async_copy(values_ref.at[span], values.at[span], sems.at[i]) for i, span in enumerate(spans)]
    copies.append(pltpu.make_async_copy(cluster_ref, cluster, sems.at[PARTS]))
    copies.append(pltpu.make_async_copy(order_ref, order, sems.at[PARTS + 1]))
    for copy in copies:
        copy.start()
    for i in range(PARTS):
        copies[i].wait()
        part = values[i * step : (i + 1) * step, :].astype(F32)
        unit = part * lax.rsqrt(jnp.sum(part * part, axis=1, keepdims=True) + 1e-06)
        full_ref[i * step : (i + 1) * step, :] = unit.astype(BF16)
    copies[PARTS].wait()
    copies[PARTS + 1].wait()
    orders = order[...]
    kept = [orders & 127, (orders >> 7) & 127, orders >> 14, cluster[...] + 1]
    kept += [jnp.zeros_like(orders)] * (KEYS - len(kept))
    keys = jnp.concatenate(kept, axis=0).astype(F32).astype(BF16)
    if width > rows:
        keys = jnp.concatenate([keys, jnp.zeros((KEYS, width - rows), BF16)], axis=1)
    full_ref[rows : rows + KEYS, :] = keys


def pack(values, cluster, order):
    rows, width = values.shape
    held = [pltpu.with_memory_space_constraint(x, pltpu.HBM) for x in (values, cluster, order)]
    return pl.pallas_call(
        pack_kernel,
        out_shape=jax.ShapeDtypeStruct((rows + KEYS, width), BF16),
        in_specs=[pl.BlockSpec(memory_space=pltpu.HBM)] * 3,
        scratch_shapes=[
            pltpu.VMEM(values.shape, BF16),
            pltpu.VMEM(cluster.shape, jnp.int32),
            pltpu.VMEM(order.shape, jnp.int32),
            pltpu.SemaphoreType.DMA((PARTS + 2,)),
        ],
        compiler_params=pltpu.CompilerParams(vmem_limit_bytes=VMEM_LIMIT),
        name="pack",
    )(*held)


def row_range(arrays, parts, low, count):
    taken = []
    for array, first, rows in parts:
        begin, end = max(low, 0), min(low + count, rows)
        if begin < end:
            taken.append((array, slice(first + begin, first + end)))
        low -= rows

    def read():
        held = [arrays[array][rows, :] for array, rows in taken]
        return held[0] if len(held) == 1 else jnp.concatenate(held, axis=0)

    return read


def pair_kernel(plan, *refs):
    n_arrays, ms, ps, sides = plan
    arrays, best_ref, out_ref = refs[:n_arrays], refs[n_arrays], refs[n_arrays + 1]
    out_ref[...] = best_ref[...]
    keys = {}
    for keyed, first in [piece[3:5] for piece in ms] + [block[1:3] for block in ps]:
        if (keyed, first) not in keys:
            keys[keyed, first] = digits(arrays[keyed], first)
    tiles = []
    for parts, keyed, first, line in ps:
        order, cluster = keys[keyed, first]
        rows = sum(count for _, _, count in parts)
        tile = min(256, rows)
        for low in range(0, rows, tile):
            span = slice(low, low + tile)
            tiles.append([row_range(arrays, parts, low, tile), order[:, span], cluster[:, span], line, span, tile])
            tiles[-1].append(jnp.full((8, tile), -1.0, F32))
    for (m, start, count, keyed, first, at, line), both in zip(ms, sides):
        order, cluster = (columns(row[:, at : at + count], count) for row in keys[keyed, first])
        m_rows = arrays[m][start : start + count, :]
        m_best = jnp.full((count, 128), -1.0, F32)
        for held in tiles:
            p_rows, p_order, p_cluster, _, _, tile, p_best = held
            scores = lax.dot_general(m_rows, p_rows(), (((1,), (1,)), ((), ())), preferred_element_type=F32)
            scores = jnp.where(cluster == p_cluster, scores, -1.0)
            later = order > p_order
            mine = jnp.where(later, scores, -1.0)
            for c in range(0, tile, 128):
                m_best = jnp.maximum(m_best, mine[:, c : c + 128])
            if both:
                other = jnp.where(later, -1.0, scores).reshape(count // 8, 8, tile)
                held[-1] = jnp.maximum(p_best, jnp.max(other, axis=0))
        m_line = jnp.max(jnp.transpose(m_best), axis=0, keepdims=True)
        span = slice(at, at + count)
        out_ref[line : line + 1, span] = jnp.maximum(out_ref[line : line + 1, span], m_line)
    if any(sides):
        for _, _, _, line, span, _, p_best in tiles:
            p_line = jnp.max(p_best, axis=0, keepdims=True)
            out_ref[line : line + 1, span] = jnp.maximum(out_ref[line : line + 1, span], p_line)


def fold(best, ms, ps, name):
    arrays = []

    def place(array):
        for at, held in enumerate(arrays):
            if held is array:
                return at
        arrays.append(array)
        return len(arrays) - 1

    m_plan = [(place(m[0]), *m[1:3], place(m[3]), *m[4:7]) for m in ms]
    p_plan = [([(place(a), *rest) for a, *rest in p[0]], place(p[1]), *p[2:]) for p in ps]
    plan = (m_plan, p_plan, [m[-1] for m in ms])
    return pl.pallas_call(
        functools.partial(pair_kernel, (len(arrays), *plan)),
        out_shape=jax.ShapeDtypeStruct(best.shape, F32),
        compiler_params=pltpu.CompilerParams(vmem_limit_bytes=VMEM_LIMIT),
        cost_estimate=pl.CostEstimate(flops=0, bytes_accessed=0, transcendentals=0),
        name=name,
    )(*arrays, best)


def after(x, *others):
    return lax.optimization_barrier((x, *others))[0]


def on_device(embeddings, cluster_ids, row_order):
    rows = embeddings.shape[0]
    n_bulk, n_grp = lax.axis_size("bulk"), lax.axis_size("grp")
    planes = n_grp // 2
    axes = ("bulk", "grp")

    def bulk_move(x, mask):
        pairs = [(b * n_grp + g, (b ^ mask) * n_grp + g) for b in range(n_bulk) for g in range(n_grp)]
        return lax.ppermute(x, axes, pairs)

    def core_move(x):
        pairs = [(b * n_grp + g, b * n_grp + (g ^ 1)) for b in range(n_bulk) for g in range(n_grp)]
        return lax.ppermute(x, axes, pairs)

    def plane_move(x, members):
        pairs = [
            (b * n_grp + 2 * s + c, b * n_grp + 2 * d + c) for b in range(n_bulk) for s, d in members for c in range(2)
        ]
        return lax.ppermute(x, axes, pairs)

    rounds = plane_rounds(planes)
    n_rounds = len(rounds)
    half, near_cut, cut = rows // 2, rows // 2, 3 * rows // 8
    last = n_bulk - 1
    full = pack(embeddings, cluster_ids.reshape(1, rows), row_order.reshape(1, rows))

    own_line, t_line = 0, 1
    z_line, tz_line = lambda k: 2 + 2 * k, lambda k: 3 + 2 * k
    p_line = lambda j: 2 + 2 * n_rounds + j
    best = jnp.full((-(-p_line(n_bulk) // 8) * 8, rows), -1.0, F32)

    def whole(x, line, both):
        return x, 0, rows, x, rows, 0, line, both

    def block(x, line):
        return [(x, 0, rows)], x, rows, line

    def go_home(lines, k):
        back = {(d, s) for s, d in rounds[k]}
        if len(back) < planes:
            back |= {(s, d) for d, s in back}
        return plane_move(lines, sorted(back))

    twin = core_move(full)
    z = [plane_move(full, members) for members in rounds]
    bulk = [bulk_move(full, mask) for mask in range(1, last)]
    same = [whole(full, own_line, False), whole(twin, t_line, False)]
    blocks = [block(full, p_line(0))]
    best = fold(best, same, blocks, "own")
    bulk = [full] + bulk
    d_top = bulk_move(bulk[1][:near_cut], last ^ 1)
    d_end = bulk_move(bulk[last ^ 1][near_cut:], 1)
    k = n_rounds - 1
    z_twin = [(core_move(x[:cut]), core_move(x[cut:])) for x in z[:k]]
    near = [block(bulk[j], p_line(j)) for j in range(1, last)]
    far = [([(d_top, 0, near_cut), (d_end, 0, rows - near_cut)], d_end, rows - near_cut, p_line(last))]
    most = []
    for r in range(k):
        top, end = z_twin[r]
        most.append(whole(z[r], z_line(r), True))
        most.append((end, 0, rows - cut, end, rows - cut, cut, tz_line(r), True))
        most.append((top, 0, cut, end, rows - cut, 0, tz_line(r), True))
    for j in range(len(near)):
        best = fold(best, same, near[j : j + 1], "near")
    best = fold(best, most, blocks + near, "column")
    best = fold(best, same + most, far, "far")

    parts = [go_home(best[z_line(r) : tz_line(r) + 1], r) for r in range(k)]
    blocks += near + far
    z_last = after(z[k], best)
    z_last_twin = core_move(z_last)
    best = fold(best, [whole(z_last, z_line(k), True)], blocks, "last")
    best = fold(best, [whole(z_last_twin, tz_line(k), True)], blocks, "rest")

    parts.append(go_home(best[z_line(k) : tz_line(k) + 1], k))
    both = functools.reduce(jnp.maximum, parts, best[own_line : t_line + 1])
    mine = best[p_line(0)]
    for j in range(1, last):
        mine = jnp.maximum(mine, bulk_move(best[p_line(j)], j))
    mine = jnp.maximum(mine, bulk_move(best, last)[p_line(last)])
    return jnp.maximum(jnp.maximum(both[0], core_move(both[1])), mine)


def solution(mesh):
    return jax.shard_map(
        on_device,
        mesh=mesh,
        in_specs=(P(("bulk", "grp"), None), P(("bulk", "grp"), None), P(("bulk", "grp"))),
        out_specs=P(("bulk", "grp")),
        check_vma=False,
    )
```

```python
import functools

import jax
import jax.numpy as jnp
from jax import lax
from jax.experimental import pallas as pl
from jax.experimental.pallas import tpu as pltpu
from jax.sharding import PartitionSpec as P

F32 = jnp.float32
BF16 = jnp.bfloat16
KEYS = 16
PARTS = 4
VMEM_LIMIT = 32 * 1024 * 1024


def plane_rounds(planes):
    rounds = [[(z, (z - k) % planes) for z in range(planes)] for k in range(1, (planes + 1) // 2)]
    if planes % 2 == 0:
        half = planes // 2
        rounds.append([(z, z + half) if z % 2 == 0 else (z + half, z) for z in range(half)])
    return rounds


def digits(ref, first):
    keys = ref[pl.ds(first, KEYS), :].astype(F32)
    order = keys[0:1] + 128.0 * keys[1:2] + 16384.0 * keys[2:3]
    return order, keys[3:4]


def columns(row, length):
    return jnp.transpose(jnp.broadcast_to(row, (8, row.shape[1])))[:length, 0:1]


def pack_kernel(values_ref, cluster_ref, order_ref, full_ref, values, cluster, order, sems):
    rows, width = values_ref.shape
    step = rows // PARTS
    spans = [pl.ds(i * step, step) for i in range(PARTS)]
    copies = [pltpu.make_async_copy(values_ref.at[span], values.at[span], sems.at[i]) for i, span in enumerate(spans)]
    copies.append(pltpu.make_async_copy(cluster_ref, cluster, sems.at[PARTS]))
    copies.append(pltpu.make_async_copy(order_ref, order, sems.at[PARTS + 1]))
    for copy in copies:
        copy.start()
    for i in range(PARTS):
        copies[i].wait()
        part = values[i * step : (i + 1) * step, :].astype(F32)
        unit = part * lax.rsqrt(jnp.sum(part * part, axis=1, keepdims=True) + 1e-06)
        full_ref[i * step : (i + 1) * step, :] = unit.astype(BF16)
    copies[PARTS].wait()
    copies[PARTS + 1].wait()
    orders = order[...]
    kept = [orders & 127, (orders >> 7) & 127, orders >> 14, cluster[...] + 1]
    kept += [jnp.zeros_like(orders)] * (KEYS - len(kept))
    keys = jnp.concatenate(kept, axis=0).astype(F32).astype(BF16)
    if width > rows:
        keys = jnp.concatenate([keys, jnp.zeros((KEYS, width - rows), BF16)], axis=1)
    full_ref[rows : rows + KEYS, :] = keys


def pack(values, cluster, order):
    rows, width = values.shape
    held = [pltpu.with_memory_space_constraint(x, pltpu.HBM) for x in (values, cluster, order)]
    return pl.pallas_call(
        pack_kernel,
        out_shape=jax.ShapeDtypeStruct((rows + KEYS, width), BF16),
        in_specs=[pl.BlockSpec(memory_space=pltpu.HBM)] * 3,
        scratch_shapes=[
            pltpu.VMEM(values.shape, BF16),
            pltpu.VMEM(cluster.shape, jnp.int32),
            pltpu.VMEM(order.shape, jnp.int32),
            pltpu.SemaphoreType.DMA((PARTS + 2,)),
        ],
        compiler_params=pltpu.CompilerParams(vmem_limit_bytes=VMEM_LIMIT),
        name="pack",
    )(*held)


def row_range(arrays, parts, low, count):
    taken = []
    for array, first, rows in parts:
        begin, end = max(low, 0), min(low + count, rows)
        if begin < end:
            taken.append((array, slice(first + begin, first + end)))
        low -= rows

    def read():
        held = [arrays[array][rows, :] for array, rows in taken]
        return held[0] if len(held) == 1 else jnp.concatenate(held, axis=0)

    return read


def pair_kernel(plan, *refs):
    n_arrays, ms, ps, sides = plan
    arrays, best_ref, out_ref = refs[:n_arrays], refs[n_arrays], refs[n_arrays + 1]
    out_ref[...] = best_ref[...]
    keys = {}
    for keyed, first in [piece[3:5] for piece in ms] + [block[1:3] for block in ps]:
        if (keyed, first) not in keys:
            keys[keyed, first] = digits(arrays[keyed], first)
    tiles = []
    for parts, keyed, first, line in ps:
        order, cluster = keys[keyed, first]
        rows = sum(count for _, _, count in parts)
        tile = min(256, rows)
        for low in range(0, rows, tile):
            span = slice(low, low + tile)
            tiles.append([row_range(arrays, parts, low, tile), order[:, span], cluster[:, span], line, span, tile])
            tiles[-1].append(jnp.full((8, tile), -1.0, F32))
    for (m, start, count, keyed, first, at, line), both in zip(ms, sides):
        order, cluster = (columns(row[:, at : at + count], count) for row in keys[keyed, first])
        m_rows = arrays[m][start : start + count, :]
        m_best = jnp.full((count, 128), -1.0, F32)
        for held in tiles:
            p_rows, p_order, p_cluster, _, _, tile, p_best = held
            scores = lax.dot_general(m_rows, p_rows(), (((1,), (1,)), ((), ())), preferred_element_type=F32)
            scores = jnp.where(cluster == p_cluster, scores, -1.0)
            later = order > p_order
            mine = jnp.where(later, scores, -1.0)
            for c in range(0, tile, 128):
                m_best = jnp.maximum(m_best, mine[:, c : c + 128])
            if both:
                other = jnp.where(later, -1.0, scores).reshape(count // 8, 8, tile)
                held[-1] = jnp.maximum(p_best, jnp.max(other, axis=0))
        m_line = jnp.max(jnp.transpose(m_best), axis=0, keepdims=True)
        span = slice(at, at + count)
        out_ref[line : line + 1, span] = jnp.maximum(out_ref[line : line + 1, span], m_line)
    if any(sides):
        for _, _, _, line, span, _, p_best in tiles:
            p_line = jnp.max(p_best, axis=0, keepdims=True)
            out_ref[line : line + 1, span] = jnp.maximum(out_ref[line : line + 1, span], p_line)


def fold(best, ms, ps, name):
    arrays = []

    def place(array):
        for at, held in enumerate(arrays):
            if held is array:
                return at
        arrays.append(array)
        return len(arrays) - 1

    m_plan = [(place(m[0]), *m[1:3], place(m[3]), *m[4:7]) for m in ms]
    p_plan = [([(place(a), *rest) for a, *rest in p[0]], place(p[1]), *p[2:]) for p in ps]
    plan = (m_plan, p_plan, [m[-1] for m in ms])
    return pl.pallas_call(
        functools.partial(pair_kernel, (len(arrays), *plan)),
        out_shape=jax.ShapeDtypeStruct(best.shape, F32),
        compiler_params=pltpu.CompilerParams(vmem_limit_bytes=VMEM_LIMIT),
        cost_estimate=pl.CostEstimate(flops=0, bytes_accessed=0, transcendentals=0),
        name=name,
    )(*arrays, best)


def after(x, *others):
    return lax.optimization_barrier((x, *others))[0]


def on_device(embeddings, cluster_ids, row_order):
    rows = embeddings.shape[0]
    n_bulk, n_grp = lax.axis_size("bulk"), lax.axis_size("grp")
    planes = n_grp // 2
    axes = ("bulk", "grp")

    def bulk_move(x, mask):
        pairs = [(b * n_grp + g, (b ^ mask) * n_grp + g) for b in range(n_bulk) for g in range(n_grp)]
        return lax.ppermute(x, axes, pairs)

    def core_move(x):
        pairs = [(b * n_grp + g, b * n_grp + (g ^ 1)) for b in range(n_bulk) for g in range(n_grp)]
        return lax.ppermute(x, axes, pairs)

    def plane_move(x, members):
        pairs = [
            (b * n_grp + 2 * s + c, b * n_grp + 2 * d + c) for b in range(n_bulk) for s, d in members for c in range(2)
        ]
        return lax.ppermute(x, axes, pairs)

    rounds = plane_rounds(planes)
    n_rounds = len(rounds)
    half, near_cut, cut = rows // 2, rows // 2, 3 * rows // 8
    last = n_bulk - 1
    full = pack(embeddings, cluster_ids.reshape(1, rows), row_order.reshape(1, rows))

    own_line, t_line = 0, 1
    z_line, tz_line = lambda k: 2 + 2 * k, lambda k: 3 + 2 * k
    p_line = lambda j: 2 + 2 * n_rounds + j
    best = jnp.full((-(-p_line(n_bulk) // 8) * 8, rows), -1.0, F32)

    def whole(x, line, both):
        return x, 0, rows, x, rows, 0, line, both

    def block(x, line):
        return [(x, 0, rows)], x, rows, line

    def go_home(lines, k):
        back = {(d, s) for s, d in rounds[k]}
        if len(back) < planes:
            back |= {(s, d) for d, s in back}
        return plane_move(lines, sorted(back))

    twin = core_move(full)
    z = [plane_move(full, members) for members in rounds]
    bulk = [bulk_move(full, mask) for mask in range(1, last)]
    same = [whole(full, own_line, False), whole(twin, t_line, False)]
    blocks = [block(full, p_line(0))]
    best = fold(best, same, blocks, "own")
    bulk = [full] + bulk
    d_top = bulk_move(bulk[1][:near_cut], last ^ 1)
    d_end = bulk_move(bulk[last ^ 1][near_cut:], 1)
    k = n_rounds - 1
    z_twin = [(core_move(x[:cut]), core_move(x[cut:])) for x in z[:k]]
    near = [block(bulk[j], p_line(j)) for j in range(1, last)]
    far = [([(d_top, 0, near_cut), (d_end, 0, rows - near_cut)], d_end, rows - near_cut, p_line(last))]
    most = []
    for r in range(k):
        top, end = z_twin[r]
        most.append(whole(z[r], z_line(r), True))
        most.append((end, 0, rows - cut, end, rows - cut, cut, tz_line(r), True))
        most.append((top, 0, cut, end, rows - cut, 0, tz_line(r), True))
    best = fold(best, same, near, "near")
    best = fold(best, most, blocks + near, "column")
    best = fold(best, same + most, far, "far")

    parts = [go_home(best, r)[z_line(r) : tz_line(r) + 1] for r in range(k)]
    blocks += near + far
    z_last = after(z[k], best)
    z_last_twin = core_move(z_last)
    best = fold(best, [whole(z_last, z_line(k), True)], blocks, "last")
    best = fold(best, [whole(z_last_twin, tz_line(k), True)], blocks, "rest")

    parts.append(go_home(best[z_line(k) : tz_line(k) + 1], k))
    both = functools.reduce(jnp.maximum, parts, best[own_line : t_line + 1])
    mine = best[p_line(0)]
    for j in range(1, last):
        mine = jnp.maximum(mine, bulk_move(best[p_line(j)], j))
    mine = jnp.maximum(mine, bulk_move(best, last)[p_line(last)])
    return jnp.maximum(jnp.maximum(both[0], core_move(both[1])), mine)


def solution(mesh):
    return jax.shard_map(
        on_device,
        mesh=mesh,
        in_specs=(P(("bulk", "grp"), None), P(("bulk", "grp"), None), P(("bulk", "grp"))),
        out_specs=P(("bulk", "grp")),
        check_vma=False,
    )
```
